32 devices in a mesh: slab: 8 (over z, y), grp: 4 (over x, core).
Axes of the slice: x: 2, y: 2, z: 4, core: 2. Of those that a mesh axis runs over, the one named last changes fastest.
Arguments:
- velocity: float32 [3, 4096], P(None, ('slab', 'grp')), may hold values from -6 to 6
- grad_shape: float32 [4, 3, 16384], P(None, None, ('slab', 'grp')), may hold values from -3 to 3
- element_nodes: int32 [4, 16384], P(None, ('slab', 'grp')), may hold values from 0 to 575
- packet_element: int32 [8192], P(('slab', 'grp')), may hold values from 0 to 511
- dest_slab: int32 [8192], P(('slab', 'grp')), may hold values from 0 to 7, as said below
- live_count: int32 [32], P(('slab', 'grp')), may hold values from 64 to 256, as said below
- entangle: int32 [8192, 256], P(('slab', 'grp')), may hold values from 1 to 8
- conform: float32 [8192, 6, 256], P(('slab', 'grp')), may hold values from -6 to 6
Outputs:
- deformed: float32 [8192, 6, 256], P(('slab', 'grp'))
- nodal_force: float32 [3, 4096], P(None, ('slab', 'grp'))
- arrived: float32 [2, 1024, 6, 256], P(None, ('slab', 'grp'))
The draws below stay inside these ranges and needn't reach their ends.
Inputs may be any that keep to these rules, and one draw needn't show every extreme that they name: `dest_slab`: packets in dead slots keep their own slab; a live packet goes to its own slab or one of the two next to it; from each device at most 32 packets go to each neighbouring slab, and that many in some devices of every draw. `live_count`: at least 64 live slots on each device, all slots on some.
All inputs are finite; a program needn't handle non-finite values.
Results may differ from the reference program's by a relative error of at most 0.000088.
Values sent between devices are 32-bit elements; how exact they have to be, the bound alone decides.
A program may use at most 64 MiB of HBM per device.

```python
import jax
import jax.numpy as jnp
from jax import lax

CHAINS = 256
PK_DEV = 256
EL_DEV = 512
HALO = 64
MOVE = 32
SLABS = 8
GROUP = 4
DEVS = 32
SLAB_NODES = 512
NODES = 4096
ELEMENTS = 16384
TOTAL_PK = 8192


def packet_plan(key):
    base_key = jax.random.fold_in(key, 7)
    key_count, key_lower, key_upper, key_perm = jax.random.split(base_key, 4)
    device = jnp.arange(DEVS, dtype=jnp.int32)
    slab_of = device // GROUP
    member = device % GROUP
    counts = jax.random.randint(key_count, (DEVS,), PK_DEV // 4, PK_DEV + 1)
    counts = jnp.where(member == GROUP - 1, PK_DEV, counts)
    to_lower = jax.random.randint(key_lower, (DEVS,), MOVE // 3, MOVE + 1)
    to_lower = jnp.where(member == 0, MOVE, to_lower)
    to_lower = jnp.where(slab_of == 0, 0, to_lower)
    to_upper = jax.random.randint(key_upper, (DEVS,), MOVE // 3, MOVE + 1)
    to_upper = jnp.where(member == 1, MOVE, to_upper)
    to_upper = jnp.where(slab_of == SLABS - 1, 0, to_upper)
    perms = jax.vmap(lambda sub_key: jax.random.permutation(sub_key, PK_DEV))(jax.random.split(key_perm, DEVS))
    slots = jnp.arange(PK_DEV, dtype=jnp.int32)
    scores = jnp.where(slots[None, :] < counts[:, None], 0, PK_DEV) + perms
    order = jnp.argsort(scores, axis=1)
    ranks = jnp.argsort(order, axis=1)
    lower = (ranks < to_lower[:, None]).astype(jnp.int32)
    upper = ((ranks >= to_lower[:, None]) & (ranks < (to_lower + to_upper)[:, None])).astype(jnp.int32)
    dest = slab_of[:, None] - lower + upper
    return (counts.astype(jnp.int32), dest.reshape(-1).astype(jnp.int32))


def draw_dest_slab(key, part):
    return packet_plan(key)[1]


def draw_live_count(key, part):
    return packet_plan(key)[0]


def with_ends(values, own_key, smallest, high):
    spot = [jax.random.randint(jax.random.fold_in(own_key, axis), (), 0, length) for axis, length in enumerate(values.shape)]
    widest = values.shape.index(max(values.shape))
    neighbour = spot[:widest] + [(spot[widest] + 1) % values.shape[widest]] + spot[widest + 1:]
    return values.at[tuple(spot)].set(smallest).at[tuple(neighbour)].set(high)


def levels(stream_key, dims, cuts, low, high):
    loudness, own = 1.0, jax.random.fold_in(stream_key, 6)
    for position, blocks in cuts:
        draws = jnp.exp(jax.random.uniform(jax.random.fold_in(own, position), (blocks,), jnp.float32, low / len(cuts), high / len(cuts)))
        loudness = loudness * jnp.repeat(draws, dims[position] // blocks).reshape([-1 if axis == position else 1 for axis in range(len(dims))])
    return loudness


def scatter_about(stream_key, shape, width, bound, shards=(), kind=jnp.bfloat16):
    drawn = jax.random.normal(stream_key, shape, jnp.float32) * width
    if len(shards) > 0:
        drawn = levels(stream_key, shape, shards, -0.22, 0.18) * drawn
    return jnp.clip(drawn, min=-bound, max=bound).astype(kind)


def setup_inputs(seed: int = 0) -> dict:
    arg_keys = jax.random.split(jax.random.key(seed), 9)
    velocity = scatter_about(arg_keys[0], (3, NODES), 1.0, 6.0, ((1, 32),), jnp.float32)
    grad_shape = scatter_about(arg_keys[1], (4, 3, ELEMENTS), 4 ** -0.5, 3.0, ((2, 32),), jnp.float32)
    element_nodes = with_ends(jax.random.randint(arg_keys[2], (4, ELEMENTS), 0, SLAB_NODES + HALO), jax.random.fold_in(arg_keys[2], 1), 0, (SLAB_NODES + HALO) - 1).astype(jnp.int32)
    packet_element = with_ends(jax.random.randint(arg_keys[3], (TOTAL_PK,), 0, EL_DEV), jax.random.fold_in(arg_keys[3], 1), 0, EL_DEV - 1).astype(jnp.int32)
    dest_slab = draw_dest_slab(jax.random.fold_in(arg_keys[8], 71), 0)
    live_count = draw_live_count(jax.random.fold_in(arg_keys[8], 71), 0)
    entangle = with_ends(jax.random.randint(arg_keys[6], (TOTAL_PK, CHAINS), 1, 9), jax.random.fold_in(arg_keys[6], 1), 1, 8).astype(jnp.int32)
    conform = scatter_about(arg_keys[7], (TOTAL_PK, 6, CHAINS), 1.0, 6.0, ((0, 32),), jnp.float32)
    return {"velocity": velocity, "grad_shape": grad_shape, "element_nodes": element_nodes, "packet_element": packet_element, "dest_slab": dest_slab, "live_count": live_count, "entangle": entangle, "conform": conform}


DT = 0.1
TAU = 1.0
PAIRS = ((0, 0), (1, 1), (2, 2), (0, 1), (0, 2), (1, 2))
IDENTITY = (1.0, 1.0, 1.0, 0.0, 0.0, 0.0)
SYMMETRY = ((0, 3, 4), (3, 1, 5), (4, 5, 2))


def deform_chains(comps, vel_grad, links):
    rows = ((comps[0], comps[3], comps[4]), (comps[3], comps[1], comps[5]), (comps[4], comps[5], comps[2]))

    def product(first, second):
        return (vel_grad[first, 0][:, None] * rows[0][second] + vel_grad[first, 1][:, None] * rows[1][second]
                + vel_grad[first, 2][:, None] * rows[2][second])

    relax = DT / (TAU * links)
    result = []
    for index in range(6):
        first, second = PAIRS[index]
        result.append(comps[index] + DT * (product(first, second) + product(second, first))
                      - relax * (comps[index] - IDENTITY[index]))
    return jnp.stack(result, 1)


def reference(velocity, grad_shape, element_nodes, packet_element, dest_slab, live_count, entangle, conform):
    span = SLAB_NODES + HALO
    vel_three = velocity.reshape(3, SLABS, SLAB_NODES)
    nxt_rows = jnp.concatenate([vel_three[:, 1:, :HALO], jnp.zeros((3, 1, HALO), jnp.float32)], 1)
    extended = jnp.concatenate([vel_three, nxt_rows], 2)
    links_slab = element_nodes.reshape(4, SLABS, GROUP * EL_DEV)
    node_vel = jax.vmap(lambda ext_one, con_one: jnp.take(ext_one, con_one, axis=1), in_axes=(1, 1), out_axes=2)(extended, links_slab)
    node_vel = node_vel.reshape(3, 4, ELEMENTS)
    vel_grad = jnp.einsum('iae,aje->ije', node_vel, grad_shape, precision=lax.Precision.HIGHEST)
    global_elem = (packet_element.reshape(DEVS, PK_DEV) + jnp.arange(DEVS, dtype=jnp.int32)[:, None] * EL_DEV).reshape(-1)
    packet_grad = jnp.take(vel_grad, global_elem, axis=2)
    alive_mask = (jnp.arange(PK_DEV, dtype=jnp.int32)[None, :] < live_count[:, None]).reshape(-1)
    comps = [conform[:, index, :] for index in range(6)]
    fresh = deform_chains(comps, packet_grad, entangle.astype(jnp.float32))
    deformed = jnp.where(alive_mask[:, None, None], fresh, 0.0)
    ident = jnp.array(IDENTITY, jnp.float32)
    stress = (jnp.mean(fresh, 2) - ident[None, :]) * alive_mask[:, None].astype(jnp.float32)
    elem_stress = jax.ops.segment_sum(stress, global_elem, ELEMENTS).T
    stress_mat = elem_stress[jnp.array(SYMMETRY)]
    elem_force = -jnp.einsum('ije,aje->iae', stress_mat, grad_shape, precision=lax.Precision.HIGHEST)
    offsets = jnp.arange(SLABS, dtype=jnp.int32)[None, :, None] * span
    flat_index = (links_slab + offsets).reshape(-1)
    gathered = jnp.zeros((3, SLABS * span), jnp.float32).at[:, flat_index].add(elem_force.reshape(3, 4, SLABS, GROUP * EL_DEV).reshape(3, -1))
    gathered = gathered.reshape(3, SLABS, span)
    own_part = gathered[:, :, :SLAB_NODES]
    rim_part = gathered[:, :, SLAB_NODES:]
    moved_rim = jnp.concatenate([jnp.zeros((3, 1, HALO), jnp.float32), rim_part[:, :-1]], 1)
    own_part = own_part.at[:, :, :HALO].add(moved_rim)
    nodal_force = own_part.reshape(3, NODES)
    flat_state = deformed.reshape(DEVS, PK_DEV, 6 * CHAINS)
    targets = dest_slab.reshape(DEVS, PK_DEV)
    slab_of = jnp.arange(DEVS, dtype=jnp.int32) // GROUP
    alive_two = alive_mask.reshape(DEVS, PK_DEV)

    def bucket(selected):
        ranks = jnp.cumsum(selected.astype(jnp.int32), 1) - 1
        one_hot = ((ranks[:, None, :] == jnp.arange(MOVE, dtype=jnp.int32)[None, :, None]) & selected[:, None, :]).astype(jnp.float32)
        return jnp.einsum('dmp,dpc->dmc', one_hot, flat_state, precision=lax.Precision.HIGHEST)

    upward = bucket(alive_two & (targets == slab_of[:, None] + 1)).reshape(SLABS, GROUP, MOVE, 6, CHAINS)
    downward = bucket(alive_two & (targets == slab_of[:, None] - 1)).reshape(SLABS, GROUP, MOVE, 6, CHAINS)
    blank = jnp.zeros((1, GROUP, MOVE, 6, CHAINS), jnp.float32)
    from_lower = jnp.concatenate([blank, upward[:-1]], 0)
    from_upper = jnp.concatenate([downward[1:], blank], 0)
    arrived = jnp.stack([from_lower, from_upper]).reshape(2, DEVS * MOVE, 6, CHAINS)
    return (deformed, nodal_force, arrived)
```

```python
import functools

import jax
import jax.numpy as jnp
from jax import lax
from jax.experimental import pallas as pl
from jax.experimental.pallas import tpu as pltpu
from jax.sharding import PartitionSpec as P

MOVE = 32
DT = 0.1
TAU = 1.0
PAIRS = ((0, 0), (1, 1), (2, 2), (0, 1), (0, 2), (1, 2))
IDENTITY = (1.0, 1.0, 1.0, 0.0, 0.0, 0.0)
SYMMETRY = ((0, 3, 4), (3, 1, 5), (4, 5, 2))
MESH = pl.DeviceIdType.MESH
F32, BF16 = jnp.float32, jnp.bfloat16
ROWS = 16


def halves(x):
    high = x.astype(BF16)
    return high, (x - high.astype(F32)).astype(BF16)


def dot(a, b):
    return jnp.dot(a, b, preferred_element_type=F32)


def deform(comps, grad, relax):
    result = []
    for index, (i, j) in enumerate(PAIRS):
        first = sum(grad[i][k] * comps[SYMMETRY[k][j]] for k in range(3))
        if i == j:
            change = first + first
        else:
            change = first + sum(grad[j][k] * comps[SYMMETRY[k][i]] for k in range(3))
        off = comps[index] - 1.0 if IDENTITY[index] else comps[index]
        result.append(comps[index] + change - relax * off)
    return result


def kernel(
    slabs, group,
    vel_ref, shape_ref, nodes_ref, elem_ref, dest_ref, live_ref, ent_hbm, con_hbm,
    out_ref, force_ref, arr_ref,
    con, ent, relax, table, node_hot, vel_all, vel_mat, grad_rows, grad_cols, sums,
    force_mat, part, landed, rim, bucket_hot, bucket_in, bucket_out,
    local_sem, vel_send, halo_send, vel_recv, part_send, part_recv, rim_send, rim_recv,
    move_send, move_recv,
):
    s, g = lax.axis_index("slab"), lax.axis_index("grp")
    width = vel_ref.shape[1]
    slots, chains = ent_hbm.shape
    elems = nodes_ref.shape[1]
    span = node_hot.shape[0]
    has_next, has_prev = s < slabs - 1, s > 0

    con_copy = pltpu.make_async_copy(con_hbm, con, local_sem.at[0])
    ent_copy = pltpu.make_async_copy(ent_hbm, ent, local_sem.at[1])
    con_copy.start()
    ent_copy.start()

    barrier = pltpu.get_barrier_semaphore()

    def greet(slab, member):
        pl.semaphore_signal(barrier, inc=1, device_id=(slab, member), device_id_type=MESH)

    for off in range(1, group):
        greet(s, lax.rem(g + off, group))

    @pl.when(has_next)
    def _():
        greet(s + 1, g)

        @pl.when(g > 0)
        def _():
            greet(s + 1, 0)

    @pl.when(has_prev)
    def _():
        greet(s - 1, g)

        @pl.when(g == 0)
        def _():
            for member in range(1, group):
                greet(s - 1, member)

    up, down = jnp.where(has_next, 1, 0), jnp.where(has_prev, 1, 0)
    pl.semaphore_wait(barrier, group - 1 + up + down + jnp.where(g == 0, (group - 1) * down, up))

    def vel_copy(slab, member, slot, send, recv):
        return pltpu.make_async_remote_copy(
            vel_ref, vel_all.at[slot], send, recv, device_id=(slab, member), device_id_type=MESH
        )

    for off in range(1, group):
        vel_copy(s, lax.rem(g + off, group), g, vel_send.at[off], vel_recv.at[g]).start()

    @pl.when(has_prev & (g == 0))
    def _():
        for member in range(group):
            vel_copy(s - 1, member, group, halo_send.at[member], vel_recv.at[group]).start()

    vel_all[g] = vel_ref[...]

    @pl.when(jnp.logical_not(has_next))
    def _():
        vel_all[group] = jnp.zeros_like(vel_ref)
        arr_ref[1] = jnp.zeros_like(arr_ref[1])

    @pl.when(jnp.logical_not(has_prev))
    def _():
        arr_ref[0] = jnp.zeros_like(arr_ref[0])

    table[...] = jnp.zeros_like(table)
    for j in range(3):
        high, low = halves(shape_ref[j])
        table[4 * j:4 * j + 4] = high.astype(F32)
        table[16 + 4 * j:20 + 4 * j] = low.astype(F32)
    nodes = nodes_ref[...]
    table[32:36] = (nodes >> 8).astype(F32)
    table[40:44] = (nodes & 255).astype(F32)
    elem_hot = (lax.broadcasted_iota(jnp.int32, (elems, slots), 0) == elem_ref[...]).astype(F32).astype(BF16)
    picked = dot(table[...].astype(BF16), elem_hot)
    shape = picked[0:12] + picked[16:28]
    index = 256.0 * picked[32:36] + picked[40:44]
    node_id = lax.broadcasted_iota(jnp.int32, (span, slots), 0).astype(F32)
    for a in range(4):
        node_hot[:, a * slots:(a + 1) * slots] = (node_id == index[a:a + 1]).astype(F32).astype(BF16)

    live = live_ref[0]
    alive = lax.broadcasted_iota(jnp.int32, (1, slots), 1) < live
    dest = dest_ref[...]
    goes = [jnp.where(alive & (dest == s + step), 1.0, 0.0) for step in (1, -1)]
    both = jnp.concatenate([jnp.broadcast_to(x, (8, slots)) for x in goes], 0)
    before = lax.broadcasted_iota(jnp.int32, (slots, slots), 0) <= lax.broadcasted_iota(jnp.int32, (slots, slots), 1)
    rank = dot(both.astype(BF16), before.astype(F32).astype(BF16))
    place = (lax.broadcasted_iota(jnp.int32, (MOVE, slots), 0) + 1).astype(F32)
    for way in range(2):
        hot = jnp.where(rank[8 * way:8 * way + 1] == place, goes[way], 0.0)
        bucket_hot[way * MOVE:(way + 1) * MOVE] = hot.astype(BF16)

    con_copy.wait()
    ent_copy.wait()
    hot = bucket_hot[...]
    entangled = ent[...].astype(F32)
    relax[...] = DT / (TAU * entangled)
    links = dot(hot, entangled.astype(BF16))
    bucket_in[6] = jnp.where(links > 0.0, DT / (TAU * jnp.maximum(links, 1.0)), 0.0)
    sums[...] = jnp.zeros_like(sums)
    for c in range(6):
        block = con[c]
        high, low = halves(block)
        bucket_in[c] = dot(hot, high) + dot(hot, low)
        off = block - 1.0 if IDENTITY[c] else block
        sums[:, c:c + 1] = jnp.sum(block, 1, keepdims=True)
        sums[:, 8 + c:9 + c] = jnp.sum(relax[...] * off, 1, keepdims=True)
    means = sums[...].T * (1.0 / chains)
    grad_rows[...] = jnp.zeros_like(grad_rows)
    vel_mat[...] = jnp.zeros_like(vel_mat)
    force_mat[...] = jnp.zeros_like(force_mat)

    for off in range(1, group):
        source = lax.rem(g + group - off, group)
        vel_copy(s, source, source, vel_send.at[off], vel_recv.at[source]).wait_recv()

    @pl.when(has_next)
    def _():
        vel_copy(s + 1, 0, group, halo_send.at[0], vel_recv.at[group]).wait_recv()

    for slot in range(group + 1):
        high, low = halves(vel_all[slot])
        vel_mat[0:3, slot * width:(slot + 1) * width] = high.astype(F32)
        vel_mat[8:11, slot * width:(slot + 1) * width] = low.astype(F32)
    node_vel = dot(vel_mat[...].astype(BF16), node_hot[...])
    node_vel = node_vel[0:3] + node_vel[8:11]
    for j in range(3):
        column = sum(
            node_vel[:, a * slots:(a + 1) * slots] * shape[4 * j + a:4 * j + a + 1] for a in range(4)
        )
        grad_rows[3 * j:3 * j + 3] = DT * column
    grads = grad_rows[...]
    columns = grads.T
    grad_cols[...] = columns

    high, low = halves(columns)
    moving = dot(hot, high) + dot(hot, low)
    for way in range(2):
        rows = slice(way * MOVE, (way + 1) * MOVE)
        here = moving[rows]
        grad = [[here[:, 3 * j + i:3 * j + i + 1] for j in range(3)] for i in range(3)]
        fresh = deform([bucket_in[c, rows] for c in range(6)], grad, bucket_in[6, rows])
        for c in range(6):
            bucket_out[way, c] = fresh[c]

    def move(way, slab):
        return pltpu.make_async_remote_copy(
            bucket_out.at[way], arr_ref.at[way], move_send.at[way], move_recv.at[way],
            device_id=(slab, g), device_id_type=MESH,
        )

    @pl.when(has_next)
    def _():
        move(0, s + 1).start()

    @pl.when(has_prev)
    def _():
        move(1, s - 1).start()

    grad = [[grads[3 * j + i:3 * j + i + 1] for j in range(3)] for i in range(3)]
    mean = [means[c:c + 1] for c in range(6)]
    stress = []
    for c, (i, j) in enumerate(PAIRS):
        first = sum(grad[i][k] * mean[SYMMETRY[k][j]] for k in range(3))
        second = sum(grad[j][k] * mean[SYMMETRY[k][i]] for k in range(3))
        value = mean[c] + (first + second) - means[8 + c:9 + c] - IDENTITY[c]
        stress.append(jnp.where(alive, value, 0.0))
    for i in range(3):
        for a in range(4):
            pull = -sum(stress[SYMMETRY[i][j]] * shape[4 * j + a:4 * j + a + 1] for j in range(3))
            high, low = halves(pull)
            force_mat[i:i + 1, a * slots:(a + 1) * slots] = high.astype(F32)
            force_mat[8 + i:9 + i, a * slots:(a + 1) * slots] = low.astype(F32)
    total = lax.dot_general(
        force_mat[...].astype(BF16), node_hot[...], (((1,), (1,)), ((), ())), preferred_element_type=F32
    )
    total = total[0:3] + total[8:11]
    for slot in range(group + 1):
        part[slot] = total[:, slot * width:(slot + 1) * width]

    def part_copy(member, source_slot, landing, send):
        return pltpu.make_async_remote_copy(
            part.at[source_slot], landed.at[landing], send, part_recv.at[landing],
            device_id=(s, member), device_id_type=MESH,
        )

    def rim_copy(slab, landing):
        return pltpu.make_async_remote_copy(
            part.at[group], rim.at[landing], rim_send.at[0], rim_recv.at[landing],
            device_id=(slab, 0), device_id_type=MESH,
        )

    @pl.when(has_next)
    def _():
        rim_copy(s + 1, g).start()

    for off in range(1, group):
        member = lax.rem(g + off, group)
        part_copy(member, member, g, part_send.at[off]).start()

    def chunk(step, carry):
        rows = pl.ds(pl.multiple_of(step * ROWS, ROWS), ROWS)
        here = grad_cols[rows]
        grad = [[here[:, 3 * j + i:3 * j + i + 1] for j in range(3)] for i in range(3)]
        fresh = deform([con[c, rows] for c in range(6)], grad, relax[rows])
        keep = lax.broadcasted_iota(jnp.int32, (ROWS, chains), 0) + step * ROWS < live
        for c in range(6):
            out_ref[c, rows] = jnp.where(keep, fresh[c], 0.0)
        return carry

    lax.fori_loop(0, slots // ROWS, chunk, 0)

    nodal = part[g]
    for off in range(1, group):
        source = lax.rem(g + group - off, group)
        part_copy(source, source, source, part_send.at[off]).wait_recv()
        nodal = nodal + landed[source]
    force_ref[...] = nodal

    @pl.when(has_prev & (g == 0))
    def _():
        more = force_ref[...]
        for member in range(group):
            rim_copy(s - 1, member).wait_recv()
            more = more + rim[member]
        force_ref[...] = more

    @pl.when(has_prev)
    def _():
        move(0, s - 1).wait_recv()
        move(1, s - 1).wait_send()

    @pl.when(has_next)
    def _():
        move(1, s + 1).wait_recv()
        move(0, s + 1).wait_send()
        rim_copy(s + 1, g).wait_send()

    for off in range(1, group):
        member = lax.rem(g + off, group)
        vel_copy(s, member, g, vel_send.at[off], vel_recv.at[g]).wait_send()
        part_copy(member, member, g, part_send.at[off]).wait_send()

    @pl.when(has_prev & (g == 0))
    def _():
        for member in range(group):
            vel_copy(s - 1, member, group, halo_send.at[member], vel_recv.at[group]).wait_send()


def shards(slabs, group, velocity, grad_shape, element_nodes, packet_element, dest_slab, live_count, entangle, conform):
    slots, chains = entangle.shape
    width = velocity.shape[1]
    span = (group + 1) * width
    vmem = pl.BlockSpec(memory_space=pltpu.VMEM)
    smem = pl.BlockSpec(memory_space=pltpu.SMEM)
    hbm = pl.BlockSpec(memory_space=pl.ANY)
    dma = pltpu.SemaphoreType.DMA
    out, force, arrived = pl.pallas_call(
        functools.partial(kernel, slabs, group),
        out_shape=(
            jax.ShapeDtypeStruct((6, slots, chains), F32),
            jax.ShapeDtypeStruct(velocity.shape, F32),
            jax.ShapeDtypeStruct((2, 6, MOVE, chains), F32),
        ),
        in_specs=[vmem, vmem, vmem, vmem, vmem, smem, hbm, hbm],
        out_specs=(vmem, vmem, vmem),
        scratch_shapes=[
            pltpu.VMEM((6, slots, chains), F32),
            pltpu.VMEM((slots, chains), jnp.int32),
            pltpu.VMEM((slots, chains), F32),
            pltpu.VMEM((48, element_nodes.shape[1]), F32),
            pltpu.VMEM((span, 4 * slots), BF16),
            pltpu.VMEM((group + 1, 3, width), F32),
            pltpu.VMEM((16, span), F32),
            pltpu.VMEM((128, slots), F32),
            pltpu.VMEM((slots, 128), F32),
            pltpu.VMEM((slots, 128), F32),
            pltpu.VMEM((16, 4 * slots), F32),
            pltpu.VMEM((group + 1, 3, width), F32),
            pltpu.VMEM((group, 3, width), F32),
            pltpu.VMEM((group, 3, width), F32),
            pltpu.VMEM((2 * MOVE, slots), BF16),
            pltpu.VMEM((7, 2 * MOVE, chains), F32),
            pltpu.VMEM((2, 6, MOVE, chains), F32),
            dma((2,)), dma((group,)), dma((group,)), dma((group + 1,)), dma((group,)), dma((group,)),
            dma((1,)), dma((group,)), dma((2,)), dma((2,)),
        ],
        compiler_params=pltpu.CompilerParams(
            collective_id=0, has_side_effects=True, vmem_limit_bytes=24 * 2**20
        ),
    )(
        velocity, grad_shape.transpose(1, 0, 2), element_nodes, packet_element.reshape(1, slots),
        dest_slab.reshape(1, slots), live_count, entangle, conform.transpose(1, 0, 2),
    )
    return out.transpose(1, 0, 2), force, arrived.transpose(0, 2, 1, 3)


def solution(mesh):
    both = ("slab", "grp")
    in_specs = (
        P(None, both), P(None, None, both), P(None, both), P(both), P(both), P(both),
        P(both, None), P(both, None, None),
    )
    out_specs = (P(both, None, None), P(None, both), P(None, both, None, None))
    body = functools.partial(shards, mesh.shape["slab"], mesh.shape["grp"])
    return jax.shard_map(body, mesh=mesh, in_specs=in_specs, out_specs=out_specs, check_vma=False)
```

```python
import functools

import jax
import jax.numpy as jnp
from jax import lax
from jax.experimental import pallas as pl
from jax.experimental.pallas import tpu as pltpu
from jax.sharding import PartitionSpec as P

MOVE = 32
DT = 0.1
TAU = 1.0
PAIRS = ((0, 0), (1, 1), (2, 2), (0, 1), (0, 2), (1, 2))
IDENTITY = (1.0, 1.0, 1.0, 0.0, 0.0, 0.0)
SYMMETRY = ((0, 3, 4), (3, 1, 5), (4, 5, 2))
MESH = pl.DeviceIdType.MESH
F32, BF16 = jnp.float32, jnp.bfloat16
ROWS = 16


def halves(x):
    high = x.astype(BF16)
    return high, (x - high.astype(F32)).astype(BF16)


def dot(a, b):
    return jnp.dot(a, b, preferred_element_type=F32)


def deform(comps, grad, relax):
    result = []
    for index, (i, j) in enumerate(PAIRS):
        first = sum(grad[i][k] * comps[SYMMETRY[k][j]] for k in range(3))
        if i == j:
            change = first + first
        else:
            change = first + sum(grad[j][k] * comps[SYMMETRY[k][i]] for k in range(3))
        off = comps[index] - 1.0 if IDENTITY[index] else comps[index]
        result.append(comps[index] + change - relax * off)
    return result


def kernel(
    slabs, group,
    vel_ref, shape_hbm, nodes_hbm, elem_hbm, dest_hbm, live_ref, ent_hbm, con_hbm,
    out_ref, force_ref, arr_ref,
    con, ent, shape_ref, nodes_ref, elem_ref, dest_ref, relax, table, node_hot, vel_all, vel_mat, grad_rows, grad_cols, sums,
    force_mat, part, landed, rim, bucket_hot, bucket_in, bucket_out,
    local_sem, vel_send, halo_send, vel_recv, part_send, part_recv, rim_send, rim_recv,
    move_send, move_recv,
):
    s, g = lax.axis_index("slab"), lax.axis_index("grp")
    width = vel_ref.shape[1]
    slots, chains = ent_hbm.shape
    elems = nodes_hbm.shape[1]
    span = node_hot.shape[0]
    has_next, has_prev = s < slabs - 1, s > 0

    arrays = (
        (elem_hbm, elem_ref), (shape_hbm, shape_ref), (nodes_hbm, nodes_ref), (vel_ref, vel_all.at[g]),
        (dest_hbm, dest_ref), (ent_hbm, ent), (con_hbm, con),
    )
    fetches = [pltpu.make_async_copy(a, b, local_sem.at[i]) for i, (a, b) in enumerate(arrays)]
    for fetch in fetches:
        fetch.start()

    barrier = pltpu.get_barrier_semaphore()

    def greet(slab, member):
        pl.semaphore_signal(barrier, inc=1, device_id=(slab, member), device_id_type=MESH)

    for off in range(1, group):
        greet(s, lax.rem(g + off, group))

    @pl.when(has_next)
    def _():
        greet(s + 1, g)

        @pl.when(g > 0)
        def _():
            greet(s + 1, 0)

    @pl.when(has_prev)
    def _():
        greet(s - 1, g)

        @pl.when(g == 0)
        def _():
            for member in range(1, group):
                greet(s - 1, member)

    table[...] = jnp.zeros_like(table)
    for fetch in fetches[:3]:
        fetch.wait()
    for j in range(3):
        high, low = halves(shape_ref[j])
        table[4 * j:4 * j + 4] = high.astype(F32)
        table[16 + 4 * j:20 + 4 * j] = low.astype(F32)
    nodes = nodes_ref[...]
    table[32:36] = (nodes >> 8).astype(F32)
    table[40:44] = (nodes & 255).astype(F32)
    elem_hot = (lax.broadcasted_iota(jnp.int32, (elems, slots), 0) == elem_ref[...]).astype(F32).astype(BF16)
    picked = dot(table[...].astype(BF16), elem_hot)
    shape = picked[0:12] + picked[16:28]
    index = 256.0 * picked[32:36] + picked[40:44]
    node_id = lax.broadcasted_iota(jnp.int32, (span, slots), 0).astype(F32)
    for a in range(4):
        node_hot[:, a * slots:(a + 1) * slots] = (node_id == index[a:a + 1]).astype(F32).astype(BF16)

    up, down = jnp.where(has_next, 1, 0), jnp.where(has_prev, 1, 0)
    pl.semaphore_wait(barrier, group - 1 + up + down + jnp.where(g == 0, (group - 1) * down, up))

    def vel_copy(slab, member, slot, send, recv):
        return pltpu.make_async_remote_copy(
            vel_ref, vel_all.at[slot], send, recv, device_id=(slab, member), device_id_type=MESH
        )

    for off in range(1, group):
        vel_copy(s, lax.rem(g + off, group), g, vel_send.at[off], vel_recv.at[g]).start()

    @pl.when(has_prev & (g == 0))
    def _():
        for member in range(group):
            vel_copy(s - 1, member, group, halo_send.at[member], vel_recv.at[group]).start()

    @pl.when(jnp.logical_not(has_next))
    def _():
        vel_all[group] = jnp.zeros(vel_ref.shape, F32)
        arr_ref[1] = jnp.zeros_like(arr_ref[1])

    @pl.when(jnp.logical_not(has_prev))
    def _():
        arr_ref[0] = jnp.zeros_like(arr_ref[0])

    fetches[4].wait()
    live = live_ref[0]
    alive = lax.broadcasted_iota(jnp.int32, (1, slots), 1) < live
    dest = dest_ref[...]
    goes = [jnp.where(alive & (dest == s + step), 1.0, 0.0) for step in (1, -1)]
    both = jnp.concatenate([jnp.broadcast_to(x, (8, slots)) for x in goes], 0)
    before = lax.broadcasted_iota(jnp.int32, (slots, slots), 0) <= lax.broadcasted_iota(jnp.int32, (slots, slots), 1)
    rank = dot(both.astype(BF16), before.astype(F32).astype(BF16))
    place = (lax.broadcasted_iota(jnp.int32, (MOVE, slots), 0) + 1).astype(F32)
    for way in range(2):
        hot = jnp.where(rank[8 * way:8 * way + 1] == place, goes[way], 0.0)
        bucket_hot[way * MOVE:(way + 1) * MOVE] = hot.astype(BF16)

    fetches[5].wait()
    fetches[6].wait()
    hot = bucket_hot[...]
    entangled = ent[...].astype(F32)
    relax[...] = DT / (TAU * entangled)
    links = dot(hot, entangled.astype(BF16))
    bucket_in[6] = jnp.where(links > 0.0, DT / (TAU * jnp.maximum(links, 1.0)), 0.0)
    sums[...] = jnp.zeros_like(sums)
    for c in range(6):
        block = con[c]
        high, low = halves(block)
        bucket_in[c] = dot(hot, high) + dot(hot, low)
        off = block - 1.0 if IDENTITY[c] else block
        sums[:, c:c + 1] = jnp.sum(block, 1, keepdims=True)
        sums[:, 8 + c:9 + c] = jnp.sum(relax[...] * off, 1, keepdims=True)
    means = sums[...].T * (1.0 / chains)
    grad_rows[...] = jnp.zeros_like(grad_rows)
    vel_mat[...] = jnp.zeros_like(vel_mat)
    force_mat[...] = jnp.zeros_like(force_mat)

    fetches[3].wait()
    for off in range(1, group):
        source = lax.rem(g + group - off, group)
        vel_copy(s, source, source, vel_send.at[off], vel_recv.at[source]).wait_recv()

    @pl.when(has_next)
    def _():
        vel_copy(s + 1, 0, group, halo_send.at[0], vel_recv.at[group]).wait_recv()

    for slot in range(group + 1):
        high, low = halves(vel_all[slot])
        vel_mat[0:3, slot * width:(slot + 1) * width] = high.astype(F32)
        vel_mat[8:11, slot * width:(slot + 1) * width] = low.astype(F32)
    node_vel = dot(vel_mat[...].astype(BF16), node_hot[...])
    node_vel = node_vel[0:3] + node_vel[8:11]
    for j in range(3):
        column = sum(
            node_vel[:, a * slots:(a + 1) * slots] * shape[4 * j + a:4 * j + a + 1] for a in range(4)
        )
        grad_rows[3 * j:3 * j + 3] = DT * column
    grads = grad_rows[...]
    columns = grads.T
    grad_cols[...] = columns

    high, low = halves(columns)
    moving = dot(hot, high) + dot(hot, low)
    for way in range(2):
        rows = slice(way * MOVE, (way + 1) * MOVE)
        here = moving[rows]
        grad = [[here[:, 3 * j + i:3 * j + i + 1] for j in range(3)] for i in range(3)]
        fresh = deform([bucket_in[c, rows] for c in range(6)], grad, bucket_in[6, rows])
        for c in range(6):
            bucket_out[way, c] = fresh[c]

    def move(way, slab):
        return pltpu.make_async_remote_copy(
            bucket_out.at[way], arr_ref.at[way], move_send.at[way], move_recv.at[way],
            device_id=(slab, g), device_id_type=MESH,
        )

    @pl.when(has_next)
    def _():
        move(0, s + 1).start()

    @pl.when(has_prev)
    def _():
        move(1, s - 1).start()

    grad = [[grads[3 * j + i:3 * j + i + 1] for j in range(3)] for i in range(3)]
    mean = [means[c:c + 1] for c in range(6)]
    stress = []
    for c, (i, j) in enumerate(PAIRS):
        first = sum(grad[i][k] * mean[SYMMETRY[k][j]] for k in range(3))
        second = sum(grad[j][k] * mean[SYMMETRY[k][i]] for k in range(3))
        value = mean[c] + (first + second) - means[8 + c:9 + c] - IDENTITY[c]
        stress.append(jnp.where(alive, value, 0.0))
    for i in range(3):
        for a in range(4):
            pull = -sum(stress[SYMMETRY[i][j]] * shape[4 * j + a:4 * j + a + 1] for j in range(3))
            high, low = halves(pull)
            force_mat[i:i + 1, a * slots:(a + 1) * slots] = high.astype(F32)
            force_mat[8 + i:9 + i, a * slots:(a + 1) * slots] = low.astype(F32)
    total = lax.dot_general(
        force_mat[...].astype(BF16), node_hot[...], (((1,), (1,)), ((), ())), preferred_element_type=F32
    )
    total = total[0:3] + total[8:11]
    for slot in range(group + 1):
        part[slot] = total[:, slot * width:(slot + 1) * width]

    def part_copy(member, source_slot, landing, send):
        return pltpu.make_async_remote_copy(
            part.at[source_slot], landed.at[landing], send, part_recv.at[landing],
            device_id=(s, member), device_id_type=MESH,
        )

    def rim_copy(slab, landing):
        return pltpu.make_async_remote_copy(
            part.at[group], rim.at[landing], rim_send.at[0], rim_recv.at[landing],
            device_id=(slab, 0), device_id_type=MESH,
        )

    @pl.when(has_next)
    def _():
        rim_copy(s + 1, g).start()

    for off in range(1, group):
        member = lax.rem(g + off, group)
        part_copy(member, member, g, part_send.at[off]).start()

    def chunk(step, carry):
        rows = pl.ds(pl.multiple_of(step * ROWS, ROWS), ROWS)
        here = grad_cols[rows]
        grad = [[here[:, 3 * j + i:3 * j + i + 1] for j in range(3)] for i in range(3)]
        fresh = deform([con[c, rows] for c in range(6)], grad, relax[rows])
        keep = lax.broadcasted_iota(jnp.int32, (ROWS, chains), 0) + step * ROWS < live
        for c in range(6):
            out_ref[c, rows] = jnp.where(keep, fresh[c], 0.0)
        return carry

    lax.fori_loop(0, slots // ROWS, chunk, 0)

    nodal = part[g]
    for off in range(1, group):
        source = lax.rem(g + group - off, group)
        part_copy(source, source, source, part_send.at[off]).wait_recv()
        nodal = nodal + landed[source]
    force_ref[...] = nodal

    @pl.when(has_prev & (g == 0))
    def _():
        more = force_ref[...]
        for member in range(group):
            rim_copy(s - 1, member).wait_recv()
            more = more + rim[member]
        force_ref[...] = more

    @pl.when(has_prev)
    def _():
        move(0, s - 1).wait_recv()
        move(1, s - 1).wait_send()

    @pl.when(has_next)
    def _():
        move(1, s + 1).wait_recv()
        move(0, s + 1).wait_send()
        rim_copy(s + 1, g).wait_send()

    for off in range(1, group):
        member = lax.rem(g + off, group)
        vel_copy(s, member, g, vel_send.at[off], vel_recv.at[g]).wait_send()
        part_copy(member, member, g, part_send.at[off]).wait_send()

    @pl.when(has_prev & (g == 0))
    def _():
        for member in range(group):
            vel_copy(s - 1, member, group, halo_send.at[member], vel_recv.at[group]).wait_send()


def pin(x):
    return pltpu.with_memory_space_constraint(x, pltpu.HBM)


def write_out(*refs):
    sem = refs[6]
    copies = [pltpu.make_async_copy(refs[i], refs[3 + i], sem.at[i]) for i in range(3)]
    for copy in copies:
        copy.start()
    for copy in copies:
        copy.wait()


def shards(slabs, group, velocity, grad_shape, element_nodes, packet_element, dest_slab, live_count, entangle, conform):
    slots, chains = entangle.shape
    width = velocity.shape[1]
    span = (group + 1) * width
    vmem = pl.BlockSpec(memory_space=pltpu.VMEM)
    hbm = pl.BlockSpec(memory_space=pltpu.HBM)
    dma = pltpu.SemaphoreType.DMA
    made = pl.pallas_call(
        functools.partial(kernel, slabs, group),
        out_shape=(
            jax.ShapeDtypeStruct((6, slots, chains), F32),
            jax.ShapeDtypeStruct(velocity.shape, F32),
            jax.ShapeDtypeStruct((2, 6, MOVE, chains), F32),
        ),
        in_specs=[hbm] * 5 + [pl.BlockSpec(memory_space=pltpu.SMEM)] + [hbm] * 2,
        out_specs=(vmem, vmem, vmem),
        scratch_shapes=[
            pltpu.VMEM((6, slots, chains), F32),
            pltpu.VMEM((slots, chains), jnp.int32),
            pltpu.VMEM((3, 4, element_nodes.shape[1]), F32),
            pltpu.VMEM(element_nodes.shape, jnp.int32),
            pltpu.VMEM((1, slots), jnp.int32),
            pltpu.VMEM((1, slots), jnp.int32),
            pltpu.VMEM((slots, chains), F32),
            pltpu.VMEM((48, element_nodes.shape[1]), F32),
            pltpu.VMEM((span, 4 * slots), BF16),
            pltpu.VMEM((group + 1, 3, width), F32),
            pltpu.VMEM((16, span), F32),
            pltpu.VMEM((128, slots), F32),
            pltpu.VMEM((slots, 128), F32),
            pltpu.VMEM((slots, 128), F32),
            pltpu.VMEM((16, 4 * slots), F32),
            pltpu.VMEM((group + 1, 3, width), F32),
            pltpu.VMEM((group, 3, width), F32),
            pltpu.VMEM((group, 3, width), F32),
            pltpu.VMEM((2 * MOVE, slots), BF16),
            pltpu.VMEM((7, 2 * MOVE, chains), F32),
            pltpu.VMEM((2, 6, MOVE, chains), F32),
            dma((7,)), dma((group,)), dma((group,)), dma((group + 1,)), dma((group,)), dma((group,)),
            dma((1,)), dma((group,)), dma((2,)), dma((2,)),
        ],
        compiler_params=pltpu.CompilerParams(
            collective_id=0, has_side_effects=True, vmem_limit_bytes=24 * 2**20
        ),
    )(
        pin(velocity), pin(grad_shape.transpose(1, 0, 2)), pin(element_nodes), pin(packet_element.reshape(1, slots)),
        pin(dest_slab.reshape(1, slots)), live_count, pin(entangle), pin(conform.transpose(1, 0, 2)),
    )
    out, force, arrived = pl.pallas_call(
        write_out,
        out_shape=[jax.ShapeDtypeStruct(x.shape, x.dtype) for x in made],
        in_specs=[vmem] * 3,
        out_specs=[hbm] * 3,
        scratch_shapes=[dma((3,))],
        compiler_params=pltpu.CompilerParams(vmem_limit_bytes=8 * 2**20),
    )(*made)
    return out.transpose(1, 0, 2), force, arrived.transpose(0, 2, 1, 3)


def solution(mesh):
    both = ("slab", "grp")
    in_specs = (
        P(None, both), P(None, None, both), P(None, both), P(both), P(both), P(both),
        P(both, None), P(both, None, None),
    )
    out_specs = (P(both, None, None), P(None, both), P(None, both, None, None))
    body = functools.partial(shards, mesh.shape["slab"], mesh.shape["grp"])
    return jax.shard_map(body, mesh=mesh, in_specs=in_specs, out_specs=out_specs, check_vma=False)
```

```python
import functools

import jax
import jax.numpy as jnp
from jax import lax
from jax.experimental import pallas as pl
from jax.experimental.pallas import tpu as pltpu
from jax.sharding import PartitionSpec as P

MOVE = 32
DT = 0.1
TAU = 1.0
PAIRS = ((0, 0), (1, 1), (2, 2), (0, 1), (0, 2), (1, 2))
IDENTITY = (1.0, 1.0, 1.0, 0.0, 0.0, 0.0)
SYMMETRY = ((0, 3, 4), (3, 1, 5), (4, 5, 2))
MESH = pl.DeviceIdType.MESH
F32, BF16 = jnp.float32, jnp.bfloat16
ROWS = 16
RAW = 16


def halves(x):
    high = x.astype(BF16)
    return high, (x - high.astype(F32)).astype(BF16)


def dot(a, b):
    return jnp.dot(a, b, preferred_element_type=F32)


def deform(comps, grad, relax):
    result = []
    for index, (i, j) in enumerate(PAIRS):
        first = sum(grad[i][k] * comps[SYMMETRY[k][j]] for k in range(3))
        if i == j:
            change = first + first
        else:
            change = first + sum(grad[j][k] * comps[SYMMETRY[k][i]] for k in range(3))
        off = comps[index] - 1.0 if IDENTITY[index] else comps[index]
        result.append(comps[index] + change - relax * off)
    return result


def kernel(
    slabs, group,
    vel_ref, shape_hbm, nodes_hbm, elem_hbm, dest_hbm, live_ref, ent_hbm, con_hbm,
    out_ref, force_ref, arr_ref,
    con, ent, shape_ref, nodes_ref, elem_ref, dest_ref, relax, table, node_hot, vel_all, vel_mat, grad_rows, grad_cols, sums,
    force_mat, part, landed, rim, bucket_hot, bucket_in, bucket_out, raw_in, grad_out, grad_in,
    local_sem, vel_send, halo_send, vel_recv, part_send, part_recv, rim_send, rim_recv,
    move_send, move_recv, raw_send, raw_recv, grad_send, grad_recv,
):
    s, g = lax.axis_index("slab"), lax.axis_index("grp")
    width = vel_ref.shape[1]
    slots, chains = ent_hbm.shape
    elems = nodes_hbm.shape[1]
    span = node_hot.shape[0]
    has_next, has_prev = s < slabs - 1, s > 0

    arrays = (
        (elem_hbm, elem_ref), (shape_hbm, shape_ref), (nodes_hbm, nodes_ref), (vel_ref, vel_all.at[g]),
        (dest_hbm, dest_ref), (ent_hbm, ent), (con_hbm, con),
    )
    fetches = [pltpu.make_async_copy(a, b, local_sem.at[i]) for i, (a, b) in enumerate(arrays)]
    for fetch in fetches:
        fetch.start()

    barrier = pltpu.get_barrier_semaphore()

    def greet(slab, member):
        pl.semaphore_signal(barrier, inc=1, device_id=(slab, member), device_id_type=MESH)

    for off in range(1, group):
        greet(s, lax.rem(g + off, group))

    @pl.when(has_next)
    def _():
        greet(s + 1, g)

        @pl.when(g > 0)
        def _():
            greet(s + 1, 0)

    @pl.when(has_prev)
    def _():
        greet(s - 1, g)

        @pl.when(g == 0)
        def _():
            for member in range(1, group):
                greet(s - 1, member)

    fetches[4].wait()
    live = live_ref[0]
    alive = lax.broadcasted_iota(jnp.int32, (1, slots), 1) < live
    dest = dest_ref[...]
    goes = [jnp.where(alive & (dest == s + step), 1.0, 0.0) for step in (1, -1)]
    both = jnp.concatenate([jnp.broadcast_to(x, (8, slots)) for x in goes], 0)
    before = lax.broadcasted_iota(jnp.int32, (slots, slots), 0) <= lax.broadcasted_iota(jnp.int32, (slots, slots), 1)
    rank = dot(both.astype(BF16), before.astype(F32).astype(BF16))
    place = (lax.broadcasted_iota(jnp.int32, (MOVE, slots), 0) + 1).astype(F32)
    for way in range(2):
        hot = jnp.where(rank[8 * way:8 * way + 1] == place, goes[way], 0.0)
        bucket_hot[way * MOVE:(way + 1) * MOVE] = hot.astype(BF16)

    fetches[5].wait()
    fetches[6].wait()
    hot = bucket_hot[...]
    entangled = ent[...].astype(F32)
    links = dot(hot, entangled.astype(BF16))
    picked_relax = jnp.where(links > 0.0, DT / (TAU * jnp.maximum(links, 1.0)), 0.0)
    for way in range(2):
        bucket_in[way, 6] = picked_relax[way * MOVE:(way + 1) * MOVE]
    for c in range(6):
        high, low = halves(con[c])
        chosen = dot(hot, high) + dot(hot, low)
        for way in range(2):
            bucket_in[way, c] = chosen[way * MOVE:(way + 1) * MOVE]

    up, down = jnp.where(has_next, 1, 0), jnp.where(has_prev, 1, 0)
    pl.semaphore_wait(barrier, group - 1 + up + down + jnp.where(g == 0, (group - 1) * down, up))

    def vel_copy(slab, member, slot, send, recv):
        return pltpu.make_async_remote_copy(
            vel_ref, vel_all.at[slot], send, recv, device_id=(slab, member), device_id_type=MESH
        )

    for off in range(1, group):
        vel_copy(s, lax.rem(g + off, group), g, vel_send.at[off], vel_recv.at[g]).start()

    @pl.when(has_prev & (g == 0))
    def _():
        for member in range(group):
            vel_copy(s - 1, member, group, halo_send.at[member], vel_recv.at[group]).start()

    def raw_copy(way, slab):
        return pltpu.make_async_remote_copy(
            bucket_in.at[way, :, 0:RAW], raw_in.at[way], raw_send.at[way], raw_recv.at[way],
            device_id=(slab, g), device_id_type=MESH,
        )

    @pl.when(has_next)
    def _():
        raw_copy(0, s + 1).start()

    @pl.when(has_prev)
    def _():
        raw_copy(1, s - 1).start()

    @pl.when(jnp.logical_not(has_next))
    def _():
        vel_all[group] = jnp.zeros(vel_ref.shape, F32)
        arr_ref[1] = jnp.zeros_like(arr_ref[1])

    @pl.when(jnp.logical_not(has_prev))
    def _():
        arr_ref[0] = jnp.zeros_like(arr_ref[0])

    table[...] = jnp.zeros_like(table)
    for fetch in fetches[:3]:
        fetch.wait()
    for j in range(3):
        high, low = halves(shape_ref[j])
        table[4 * j:4 * j + 4] = high.astype(F32)
        table[16 + 4 * j:20 + 4 * j] = low.astype(F32)
    nodes = nodes_ref[...]
    table[32:36] = (nodes >> 8).astype(F32)
    table[40:44] = (nodes & 255).astype(F32)
    elem_hot = (lax.broadcasted_iota(jnp.int32, (elems, slots), 0) == elem_ref[...]).astype(F32).astype(BF16)
    picked = dot(table[...].astype(BF16), elem_hot)
    shape = picked[0:12] + picked[16:28]
    index = 256.0 * picked[32:36] + picked[40:44]
    node_id = lax.broadcasted_iota(jnp.int32, (span, slots), 0).astype(F32)
    for a in range(4):
        node_hot[:, a * slots:(a + 1) * slots] = (node_id == index[a:a + 1]).astype(F32).astype(BF16)

    relax[...] = DT / (TAU * entangled)
    sums[...] = jnp.zeros_like(sums)
    for c in range(6):
        block = con[c]
        off = block - 1.0 if IDENTITY[c] else block
        sums[:, c:c + 1] = jnp.sum(block, 1, keepdims=True)
        sums[:, 8 + c:9 + c] = jnp.sum(relax[...] * off, 1, keepdims=True)
    means = sums[...].T * (1.0 / chains)
    grad_rows[...] = jnp.zeros_like(grad_rows)
    vel_mat[...] = jnp.zeros_like(vel_mat)
    force_mat[...] = jnp.zeros_like(force_mat)

    fetches[3].wait()
    for off in range(1, group):
        source = lax.rem(g + group - off, group)
        vel_copy(s, source, source, vel_send.at[off], vel_recv.at[source]).wait_recv()

    @pl.when(has_next)
    def _():
        vel_copy(s + 1, 0, group, halo_send.at[0], vel_recv.at[group]).wait_recv()

    for slot in range(group + 1):
        high, low = halves(vel_all[slot])
        vel_mat[0:3, slot * width:(slot + 1) * width] = high.astype(F32)
        vel_mat[8:11, slot * width:(slot + 1) * width] = low.astype(F32)
    node_vel = dot(vel_mat[...].astype(BF16), node_hot[...])
    node_vel = node_vel[0:3] + node_vel[8:11]
    for j in range(3):
        column = sum(
            node_vel[:, a * slots:(a + 1) * slots] * shape[4 * j + a:4 * j + a + 1] for a in range(4)
        )
        grad_rows[3 * j:3 * j + 3] = DT * column
    grads = grad_rows[...]
    columns = grads.T
    grad_cols[...] = columns

    high, low = halves(columns)
    moving = dot(hot, high) + dot(hot, low)

    def entries(here):
        return [[here[:, 3 * j + i:3 * j + i + 1] for j in range(3)] for i in range(3)]

    for way in range(2):
        grad_out[way] = moving[way * MOVE:way * MOVE + RAW]
        rows = slice(RAW, MOVE)
        fresh = deform(
            [bucket_in[way, c, rows] for c in range(6)],
            entries(moving[way * MOVE + RAW:(way + 1) * MOVE]), bucket_in[way, 6, rows],
        )
        for c in range(6):
            bucket_out[way, c] = fresh[c]

    def grad_copy(way, slab):
        return pltpu.make_async_remote_copy(
            grad_out.at[way], grad_in.at[way], grad_send.at[way], grad_recv.at[way],
            device_id=(slab, g), device_id_type=MESH,
        )

    def move(way, slab):
        return pltpu.make_async_remote_copy(
            bucket_out.at[way], arr_ref.at[way, :, RAW:MOVE], move_send.at[way], move_recv.at[way],
            device_id=(slab, g), device_id_type=MESH,
        )

    @pl.when(has_next)
    def _():
        grad_copy(0, s + 1).start()
        move(0, s + 1).start()

    @pl.when(has_prev)
    def _():
        grad_copy(1, s - 1).start()
        move(1, s - 1).start()

    grad = [[grads[3 * j + i:3 * j + i + 1] for j in range(3)] for i in range(3)]
    mean = [means[c:c + 1] for c in range(6)]
    stress = []
    for c, (i, j) in enumerate(PAIRS):
        first = sum(grad[i][k] * mean[SYMMETRY[k][j]] for k in range(3))
        second = sum(grad[j][k] * mean[SYMMETRY[k][i]] for k in range(3))
        value = mean[c] + (first + second) - means[8 + c:9 + c] - IDENTITY[c]
        stress.append(jnp.where(alive, value, 0.0))
    for i in range(3):
        for a in range(4):
            pull = -sum(stress[SYMMETRY[i][j]] * shape[4 * j + a:4 * j + a + 1] for j in range(3))
            high, low = halves(pull)
            force_mat[i:i + 1, a * slots:(a + 1) * slots] = high.astype(F32)
            force_mat[8 + i:9 + i, a * slots:(a + 1) * slots] = low.astype(F32)
    total = lax.dot_general(
        force_mat[...].astype(BF16), node_hot[...], (((1,), (1,)), ((), ())), preferred_element_type=F32
    )
    total = total[0:3] + total[8:11]
    for slot in range(group + 1):
        part[slot] = total[:, slot * width:(slot + 1) * width]

    def part_copy(member, source_slot, landing, send):
        return pltpu.make_async_remote_copy(
            part.at[source_slot], landed.at[landing], send, part_recv.at[landing],
            device_id=(s, member), device_id_type=MESH,
        )

    def rim_copy(slab, landing):
        return pltpu.make_async_remote_copy(
            part.at[group], rim.at[landing], rim_send.at[0], rim_recv.at[landing],
            device_id=(slab, 0), device_id_type=MESH,
        )

    @pl.when(has_next)
    def _():
        rim_copy(s + 1, g).start()

    for off in range(1, group):
        member = lax.rem(g + off, group)
        part_copy(member, member, g, part_send.at[off]).start()

    def chunk(step, carry):
        rows = pl.ds(pl.multiple_of(step * ROWS, ROWS), ROWS)
        here = grad_cols[rows]
        grad = [[here[:, 3 * j + i:3 * j + i + 1] for j in range(3)] for i in range(3)]
        fresh = deform([con[c, rows] for c in range(6)], grad, relax[rows])
        keep = lax.broadcasted_iota(jnp.int32, (ROWS, chains), 0) + step * ROWS < live
        for c in range(6):
            out_ref[c, rows] = jnp.where(keep, fresh[c], 0.0)
        return carry

    lax.fori_loop(0, slots // ROWS, chunk, 0)

    nodal = part[g]
    for off in range(1, group):
        source = lax.rem(g + group - off, group)
        part_copy(source, source, source, part_send.at[off]).wait_recv()
        nodal = nodal + landed[source]
    force_ref[...] = nodal

    @pl.when(has_prev & (g == 0))
    def _():
        more = force_ref[...]
        for member in range(group):
            rim_copy(s - 1, member).wait_recv()
            more = more + rim[member]
        force_ref[...] = more

    def finish(way, slab):
        raw_copy(way, slab).wait_recv()
        grad_copy(way, slab).wait_recv()
        fresh = deform([raw_in[way, c] for c in range(6)], entries(grad_in[way]), raw_in[way, 6])
        for c in range(6):
            arr_ref[way, c, 0:RAW] = fresh[c]
        move(way, slab).wait_recv()

    def sent(way, slab):
        raw_copy(way, slab).wait_send()
        grad_copy(way, slab).wait_send()
        move(way, slab).wait_send()

    @pl.when(has_prev)
    def _():
        finish(0, s - 1)
        sent(1, s - 1)

    @pl.when(has_next)
    def _():
        finish(1, s + 1)
        sent(0, s + 1)
        rim_copy(s + 1, g).wait_send()

    for off in range(1, group):
        member = lax.rem(g + off, group)
        vel_copy(s, member, g, vel_send.at[off], vel_recv.at[g]).wait_send()
        part_copy(member, member, g, part_send.at[off]).wait_send()

    @pl.when(has_prev & (g == 0))
    def _():
        for member in range(group):
            vel_copy(s - 1, member, group, halo_send.at[member], vel_recv.at[group]).wait_send()


def pin(x):
    return pltpu.with_memory_space_constraint(x, pltpu.HBM)


def write_out(*refs):
    sem = refs[6]
    copies = [pltpu.make_async_copy(refs[i], refs[3 + i], sem.at[i]) for i in range(3)]
    for copy in copies:
        copy.start()
    for copy in copies:
        copy.wait()


def shards(slabs, group, velocity, grad_shape, element_nodes, packet_element, dest_slab, live_count, entangle, conform):
    slots, chains = entangle.shape
    width = velocity.shape[1]
    span = (group + 1) * width
    vmem = pl.BlockSpec(memory_space=pltpu.VMEM)
    hbm = pl.BlockSpec(memory_space=pltpu.HBM)
    dma = pltpu.SemaphoreType.DMA
    made = pl.pallas_call(
        functools.partial(kernel, slabs, group),
        out_shape=(
            jax.ShapeDtypeStruct((6, slots, chains), F32),
            jax.ShapeDtypeStruct(velocity.shape, F32),
            jax.ShapeDtypeStruct((2, 6, MOVE, chains), F32),
        ),
        in_specs=[hbm] * 5 + [pl.BlockSpec(memory_space=pltpu.SMEM)] + [hbm] * 2,
        out_specs=(vmem, vmem, vmem),
        scratch_shapes=[
            pltpu.VMEM((6, slots, chains), F32),
            pltpu.VMEM((slots, chains), jnp.int32),
            pltpu.VMEM((3, 4, element_nodes.shape[1]), F32),
            pltpu.VMEM(element_nodes.shape, jnp.int32),
            pltpu.VMEM((1, slots), jnp.int32),
            pltpu.VMEM((1, slots), jnp.int32),
            pltpu.VMEM((slots, chains), F32),
            pltpu.VMEM((48, element_nodes.shape[1]), F32),
            pltpu.VMEM((span, 4 * slots), BF16),
            pltpu.VMEM((group + 1, 3, width), F32),
            pltpu.VMEM((16, span), F32),
            pltpu.VMEM((128, slots), F32),
            pltpu.VMEM((slots, 128), F32),
            pltpu.VMEM((slots, 128), F32),
            pltpu.VMEM((16, 4 * slots), F32),
            pltpu.VMEM((group + 1, 3, width), F32),
            pltpu.VMEM((group, 3, width), F32),
            pltpu.VMEM((group, 3, width), F32),
            pltpu.VMEM((2 * MOVE, slots), BF16),
            pltpu.VMEM((2, 7, MOVE, chains), F32),
            pltpu.VMEM((2, 6, MOVE - RAW, chains), F32),
            pltpu.VMEM((2, 7, RAW, chains), F32),
            pltpu.VMEM((2, RAW, 128), F32),
            pltpu.VMEM((2, RAW, 128), F32),
            dma((7,)), dma((group,)), dma((group,)), dma((group + 1,)), dma((group,)), dma((group,)),
            dma((1,)), dma((group,)), dma((2,)), dma((2,)), dma((2,)), dma((2,)), dma((2,)), dma((2,)),
        ],
        compiler_params=pltpu.CompilerParams(
            collective_id=0, has_side_effects=True, vmem_limit_bytes=24 * 2**20
        ),
    )(
        pin(velocity), pin(grad_shape.transpose(1, 0, 2)), pin(element_nodes), pin(packet_element.reshape(1, slots)),
        pin(dest_slab.reshape(1, slots)), live_count, pin(entangle), pin(conform.transpose(1, 0, 2)),
    )
    out, force, arrived = pl.pallas_call(
        write_out,
        out_shape=[jax.ShapeDtypeStruct(x.shape, x.dtype) for x in made],
        in_specs=[vmem] * 3,
        out_specs=[hbm] * 3,
        scratch_shapes=[dma((3,))],
        compiler_params=pltpu.CompilerParams(vmem_limit_bytes=8 * 2**20),
    )(*made)
    return out.transpose(1, 0, 2), force, arrived.transpose(0, 2, 1, 3)


def solution(mesh):
    both = ("slab", "grp")
    in_specs = (
        P(None, both), P(None, None, both), P(None, both), P(both), P(both), P(both),
        P(both, None), P(both, None, None),
    )
    out_specs = (P(both, None, None), P(None, both), P(None, both, None, None))
    body = functools.partial(shards, mesh.shape["slab"], mesh.shape["grp"])
    return jax.shard_map(body, mesh=mesh, in_specs=in_specs, out_specs=out_specs, check_vma=False)
```

```python
import functools

import jax
import jax.numpy as jnp
from jax import lax
from jax.experimental import pallas as pl
from jax.experimental.pallas import tpu as pltpu
from jax.sharding import PartitionSpec as P

MOVE = 32
DT = 0.1
TAU = 1.0
PAIRS = ((0, 0), (1, 1), (2, 2), (0, 1), (0, 2), (1, 2))
IDENTITY = (1.0, 1.0, 1.0, 0.0, 0.0, 0.0)
SYMMETRY = ((0, 3, 4), (3, 1, 5), (4, 5, 2))
MESH = pl.DeviceIdType.MESH
F32, BF16 = jnp.float32, jnp.bfloat16
ROWS = 16
RAW = 16


def halves(x):
    high = x.astype(BF16)
    return high, (x - high.astype(F32)).astype(BF16)


def dot(a, b):
    return jnp.dot(a, b, preferred_element_type=F32)


def deform(comps, grad, relax):
    result = []
    for index, (i, j) in enumerate(PAIRS):
        first = sum(grad[i][k] * comps[SYMMETRY[k][j]] for k in range(3))
        if i == j:
            change = first + first
        else:
            change = first + sum(grad[j][k] * comps[SYMMETRY[k][i]] for k in range(3))
        off = comps[index] - 1.0 if IDENTITY[index] else comps[index]
        result.append(comps[index] + change - relax * off)
    return result


def kernel(
    slabs, group,
    vel_ref, shape_hbm, nodes_hbm, elem_hbm, dest_hbm, live_ref, ent_hbm, con_hbm,
    out_ref, force_ref, arr_ref,
    con, ent, shape_ref, nodes_ref, elem_ref, dest_ref, relax, table, node_hot, vel_all, vel_mat, grad_rows, grad_cols, sums,
    force_mat, part, landed, rim, bucket_hot, bucket_in, bucket_out, raw_in, grad_out, grad_in,
    local_sem, vel_send, halo_send, vel_recv, part_send, part_recv, rim_send, rim_recv,
    move_send, move_recv, raw_send, raw_recv, grad_send, grad_recv,
):
    s, g = lax.axis_index("slab"), lax.axis_index("grp")
    width = vel_ref.shape[1]
    slots, chains = ent_hbm.shape
    elems = nodes_hbm.shape[1]
    span = node_hot.shape[0]
    has_next, has_prev = s < slabs - 1, s > 0

    arrays = (
        (elem_hbm, elem_ref), (shape_hbm, shape_ref), (nodes_hbm, nodes_ref), (vel_ref, vel_all.at[g]),
        (dest_hbm, dest_ref), (ent_hbm, ent), (con_hbm, con),
    )
    fetches = [pltpu.make_async_copy(a, b, local_sem.at[i]) for i, (a, b) in enumerate(arrays)]
    for fetch in fetches:
        fetch.start()

    barrier = pltpu.get_barrier_semaphore()

    def greet(slab, member):
        pl.semaphore_signal(barrier, inc=1, device_id=(slab, member), device_id_type=MESH)

    for off in range(1, group):
        greet(s, lax.rem(g + off, group))

    @pl.when(has_next)
    def _():
        greet(s + 1, g)

        @pl.when(g > 0)
        def _():
            greet(s + 1, 0)

    @pl.when(has_prev)
    def _():
        greet(s - 1, g)

        @pl.when(g == 0)
        def _():
            for member in range(1, group):
                greet(s - 1, member)

    fetches[4].wait()
    live = live_ref[0]
    alive = lax.broadcasted_iota(jnp.int32, (1, slots), 1) < live
    dest = dest_ref[...]
    goes = [jnp.where(alive & (dest == s + step), 1.0, 0.0) for step in (1, -1)]
    both = jnp.concatenate([jnp.broadcast_to(x, (8, slots)) for x in goes], 0)
    before = lax.broadcasted_iota(jnp.int32, (slots, slots), 0) <= lax.broadcasted_iota(jnp.int32, (slots, slots), 1)
    rank = dot(both.astype(BF16), before.astype(F32).astype(BF16))
    place = (lax.broadcasted_iota(jnp.int32, (MOVE, slots), 0) + 1).astype(F32)
    for way in range(2):
        hot = jnp.where(rank[8 * way:8 * way + 1] == place, goes[way], 0.0)
        bucket_hot[way * MOVE:(way + 1) * MOVE] = hot.astype(BF16)

    table[...] = jnp.zeros_like(table)
    for fetch in fetches[:3]:
        fetch.wait()
    for j in range(3):
        high, low = halves(shape_ref[j])
        table[4 * j:4 * j + 4] = high.astype(F32)
        table[16 + 4 * j:20 + 4 * j] = low.astype(F32)
    nodes = nodes_ref[...]
    table[32:36] = (nodes >> 8).astype(F32)
    table[40:44] = (nodes & 255).astype(F32)
    elem_hot = (lax.broadcasted_iota(jnp.int32, (elems, slots), 0) == elem_ref[...]).astype(F32).astype(BF16)
    picked = dot(table[...].astype(BF16), elem_hot)
    shape = picked[0:12] + picked[16:28]
    index = 256.0 * picked[32:36] + picked[40:44]
    node_id = lax.broadcasted_iota(jnp.int32, (span, slots), 0).astype(F32)
    for a in range(4):
        node_hot[:, a * slots:(a + 1) * slots] = (node_id == index[a:a + 1]).astype(F32).astype(BF16)

    fetches[5].wait()
    fetches[6].wait()
    hot = bucket_hot[...]
    entangled = ent[...].astype(F32)
    links = dot(hot, entangled.astype(BF16))
    picked_relax = jnp.where(links > 0.0, DT / (TAU * jnp.maximum(links, 1.0)), 0.0)
    for way in range(2):
        bucket_in[way, 6] = picked_relax[way * MOVE:(way + 1) * MOVE]
    for c in range(6):
        high, low = halves(con[c])
        chosen = dot(hot, high) + dot(hot, low)
        for way in range(2):
            bucket_in[way, c] = chosen[way * MOVE:(way + 1) * MOVE]

    up, down = jnp.where(has_next, 1, 0), jnp.where(has_prev, 1, 0)
    pl.semaphore_wait(barrier, group - 1 + up + down + jnp.where(g == 0, (group - 1) * down, up))

    def vel_copy(slab, member, slot, send, recv):
        return pltpu.make_async_remote_copy(
            vel_ref, vel_all.at[slot], send, recv, device_id=(slab, member), device_id_type=MESH
        )

    for off in range(1, group):
        vel_copy(s, lax.rem(g + off, group), g, vel_send.at[off], vel_recv.at[g]).start()

    @pl.when(has_prev & (g == 0))
    def _():
        for member in range(group):
            vel_copy(s - 1, member, group, halo_send.at[member], vel_recv.at[group]).start()

    def raw_copy(way, slab):
        return pltpu.make_async_remote_copy(
            bucket_in.at[way, :, 0:RAW], raw_in.at[way], raw_send.at[way], raw_recv.at[way],
            device_id=(slab, g), device_id_type=MESH,
        )

    @pl.when(has_next)
    def _():
        raw_copy(0, s + 1).start()

    @pl.when(has_prev)
    def _():
        raw_copy(1, s - 1).start()

    @pl.when(jnp.logical_not(has_next))
    def _():
        vel_all[group] = jnp.zeros(vel_ref.shape, F32)
        arr_ref[1] = jnp.zeros_like(arr_ref[1])

    @pl.when(jnp.logical_not(has_prev))
    def _():
        arr_ref[0] = jnp.zeros_like(arr_ref[0])

    relax[...] = DT / (TAU * entangled)
    sums[...] = jnp.zeros_like(sums)
    for c in range(6):
        block = con[c]
        off = block - 1.0 if IDENTITY[c] else block
        sums[:, c:c + 1] = jnp.sum(block, 1, keepdims=True)
        sums[:, 8 + c:9 + c] = jnp.sum(relax[...] * off, 1, keepdims=True)
    means = sums[...].T * (1.0 / chains)
    grad_rows[...] = jnp.zeros_like(grad_rows)
    vel_mat[...] = jnp.zeros_like(vel_mat)
    force_mat[...] = jnp.zeros_like(force_mat)

    fetches[3].wait()
    for off in range(1, group):
        source = lax.rem(g + group - off, group)
        vel_copy(s, source, source, vel_send.at[off], vel_recv.at[source]).wait_recv()

    @pl.when(has_next)
    def _():
        vel_copy(s + 1, 0, group, halo_send.at[0], vel_recv.at[group]).wait_recv()

    for slot in range(group + 1):
        high, low = halves(vel_all[slot])
        vel_mat[0:3, slot * width:(slot + 1) * width] = high.astype(F32)
        vel_mat[8:11, slot * width:(slot + 1) * width] = low.astype(F32)
    node_vel = dot(vel_mat[...].astype(BF16), node_hot[...])
    node_vel = node_vel[0:3] + node_vel[8:11]
    for j in range(3):
        column = sum(
            node_vel[:, a * slots:(a + 1) * slots] * shape[4 * j + a:4 * j + a + 1] for a in range(4)
        )
        grad_rows[3 * j:3 * j + 3] = DT * column
    grads = grad_rows[...]
    columns = grads.T
    grad_cols[...] = columns

    high, low = halves(columns)
    moving = dot(hot, high) + dot(hot, low)

    def entries(here):
        return [[here[:, 3 * j + i:3 * j + i + 1] for j in range(3)] for i in range(3)]

    for way in range(2):
        grad_out[way] = moving[way * MOVE:way * MOVE + RAW]
        rows = slice(RAW, MOVE)
        fresh = deform(
            [bucket_in[way, c, rows] for c in range(6)],
            entries(moving[way * MOVE + RAW:(way + 1) * MOVE]), bucket_in[way, 6, rows],
        )
        for c in range(6):
            bucket_out[way, c] = fresh[c]

    def grad_copy(way, slab):
        return pltpu.make_async_remote_copy(
            grad_out.at[way], grad_in.at[way], grad_send.at[way], grad_recv.at[way],
            device_id=(slab, g), device_id_type=MESH,
        )

    def move(way, slab):
        return pltpu.make_async_remote_copy(
            bucket_out.at[way], arr_ref.at[way, :, RAW:MOVE], move_send.at[way], move_recv.at[way],
            device_id=(slab, g), device_id_type=MESH,
        )

    @pl.when(has_next)
    def _():
        grad_copy(0, s + 1).start()
        move(0, s + 1).start()

    @pl.when(has_prev)
    def _():
        grad_copy(1, s - 1).start()
        move(1, s - 1).start()

    grad = [[grads[3 * j + i:3 * j + i + 1] for j in range(3)] for i in range(3)]
    mean = [means[c:c + 1] for c in range(6)]
    stress = []
    for c, (i, j) in enumerate(PAIRS):
        first = sum(grad[i][k] * mean[SYMMETRY[k][j]] for k in range(3))
        second = sum(grad[j][k] * mean[SYMMETRY[k][i]] for k in range(3))
        value = mean[c] + (first + second) - means[8 + c:9 + c] - IDENTITY[c]
        stress.append(jnp.where(alive, value, 0.0))
    for i in range(3):
        for a in range(4):
            pull = -sum(stress[SYMMETRY[i][j]] * shape[4 * j + a:4 * j + a + 1] for j in range(3))
            high, low = halves(pull)
            force_mat[i:i + 1, a * slots:(a + 1) * slots] = high.astype(F32)
            force_mat[8 + i:9 + i, a * slots:(a + 1) * slots] = low.astype(F32)
    total = lax.dot_general(
        force_mat[...].astype(BF16), node_hot[...], (((1,), (1,)), ((), ())), preferred_element_type=F32
    )
    total = total[0:3] + total[8:11]
    for slot in range(group + 1):
        part[slot] = total[:, slot * width:(slot + 1) * width]

    def part_copy(member, source_slot, landing, send):
        return pltpu.make_async_remote_copy(
            part.at[source_slot], landed.at[landing], send, part_recv.at[landing],
            device_id=(s, member), device_id_type=MESH,
        )

    def rim_copy(slab, landing):
        return pltpu.make_async_remote_copy(
            part.at[group], rim.at[landing], rim_send.at[0], rim_recv.at[landing],
            device_id=(slab, 0), device_id_type=MESH,
        )

    @pl.when(has_next)
    def _():
        rim_copy(s + 1, g).start()

    for off in range(1, group):
        member = lax.rem(g + off, group)
        part_copy(member, member, g, part_send.at[off]).start()

    def chunk(step, carry):
        rows = pl.ds(pl.multiple_of(step * ROWS, ROWS), ROWS)
        here = grad_cols[rows]
        grad = [[here[:, 3 * j + i:3 * j + i + 1] for j in range(3)] for i in range(3)]
        fresh = deform([con[c, rows] for c in range(6)], grad, relax[rows])
        keep = lax.broadcasted_iota(jnp.int32, (ROWS, chains), 0) + step * ROWS < live
        for c in range(6):
            out_ref[c, rows] = jnp.where(keep, fresh[c], 0.0)
        return carry

    lax.fori_loop(0, slots // ROWS, chunk, 0)

    nodal = part[g]
    for off in range(1, group):
        source = lax.rem(g + group - off, group)
        part_copy(source, source, source, part_send.at[off]).wait_recv()
        nodal = nodal + landed[source]
    force_ref[...] = nodal

    @pl.when(has_prev & (g == 0))
    def _():
        more = force_ref[...]
        for member in range(group):
            rim_copy(s - 1, member).wait_recv()
            more = more + rim[member]
        force_ref[...] = more

    def finish(way, slab):
        raw_copy(way, slab).wait_recv()
        grad_copy(way, slab).wait_recv()
        fresh = deform([raw_in[way, c] for c in range(6)], entries(grad_in[way]), raw_in[way, 6])
        for c in range(6):
            arr_ref[way, c, 0:RAW] = fresh[c]

    def sent(way, slab):
        raw_copy(way, slab).wait_send()
        grad_copy(way, slab).wait_send()
        move(way, slab).wait_send()

    @pl.when(has_prev)
    def _():
        finish(0, s - 1)

    @pl.when(has_next)
    def _():
        finish(1, s + 1)

    @pl.when(has_prev)
    def _():
        move(0, s - 1).wait_recv()
        sent(1, s - 1)

    @pl.when(has_next)
    def _():
        move(1, s + 1).wait_recv()
        sent(0, s + 1)
        rim_copy(s + 1, g).wait_send()

    for off in range(1, group):
        member = lax.rem(g + off, group)
        vel_copy(s, member, g, vel_send.at[off], vel_recv.at[g]).wait_send()
        part_copy(member, member, g, part_send.at[off]).wait_send()

    @pl.when(has_prev & (g == 0))
    def _():
        for member in range(group):
            vel_copy(s - 1, member, group, halo_send.at[member], vel_recv.at[group]).wait_send()


def pin(x):
    return pltpu.with_memory_space_constraint(x, pltpu.HBM)


def write_out(*refs):
    sem = refs[6]
    copies = [pltpu.make_async_copy(refs[i], refs[3 + i], sem.at[i]) for i in range(3)]
    for copy in copies:
        copy.start()
    for copy in copies:
        copy.wait()


def shards(slabs, group, velocity, grad_shape, element_nodes, packet_element, dest_slab, live_count, entangle, conform):
    slots, chains = entangle.shape
    width = velocity.shape[1]
    span = (group + 1) * width
    vmem = pl.BlockSpec(memory_space=pltpu.VMEM)
    hbm = pl.BlockSpec(memory_space=pltpu.HBM)
    dma = pltpu.SemaphoreType.DMA
    made = pl.pallas_call(
        functools.partial(kernel, slabs, group),
        out_shape=(
            jax.ShapeDtypeStruct((6, slots, chains), F32),
            jax.ShapeDtypeStruct(velocity.shape, F32),
            jax.ShapeDtypeStruct((2, 6, MOVE, chains), F32),
        ),
        in_specs=[hbm] * 5 + [pl.BlockSpec(memory_space=pltpu.SMEM)] + [hbm] * 2,
        out_specs=(vmem, vmem, vmem),
        scratch_shapes=[
            pltpu.VMEM((6, slots, chains), F32),
            pltpu.VMEM((slots, chains), jnp.int32),
            pltpu.VMEM((3, 4, element_nodes.shape[1]), F32),
            pltpu.VMEM(element_nodes.shape, jnp.int32),
            pltpu.VMEM((1, slots), jnp.int32),
            pltpu.VMEM((1, slots), jnp.int32),
            pltpu.VMEM((slots, chains), F32),
            pltpu.VMEM((48, element_nodes.shape[1]), F32),
            pltpu.VMEM((span, 4 * slots), BF16),
            pltpu.VMEM((group + 1, 3, width), F32),
            pltpu.VMEM((16, span), F32),
            pltpu.VMEM((128, slots), F32),
            pltpu.VMEM((slots, 128), F32),
            pltpu.VMEM((slots, 128), F32),
            pltpu.VMEM((16, 4 * slots), F32),
            pltpu.VMEM((group + 1, 3, width), F32),
            pltpu.VMEM((group, 3, width), F32),
            pltpu.VMEM((group, 3, width), F32),
            pltpu.VMEM((2 * MOVE, slots), BF16),
            pltpu.VMEM((2, 7, MOVE, chains), F32),
            pltpu.VMEM((2, 6, MOVE - RAW, chains), F32),
            pltpu.VMEM((2, 7, RAW, chains), F32),
            pltpu.VMEM((2, RAW, 128), F32),
            pltpu.VMEM((2, RAW, 128), F32),
            dma((7,)), dma((group,)), dma((group,)), dma((group + 1,)), dma((group,)), dma((group,)),
            dma((1,)), dma((group,)), dma((2,)), dma((2,)), dma((2,)), dma((2,)), dma((2,)), dma((2,)),
        ],
        compiler_params=pltpu.CompilerParams(
            collective_id=0, has_side_effects=True, vmem_limit_bytes=24 * 2**20
        ),
    )(
        pin(velocity), pin(grad_shape.transpose(1, 0, 2)), pin(element_nodes), pin(packet_element.reshape(1, slots)),
        pin(dest_slab.reshape(1, slots)), live_count, pin(entangle), pin(conform.transpose(1, 0, 2)),
    )
    out, force, arrived = pl.pallas_call(
        write_out,
        out_shape=[jax.ShapeDtypeStruct(x.shape, x.dtype) for x in made],
        in_specs=[vmem] * 3,
        out_specs=[hbm] * 3,
        scratch_shapes=[dma((3,))],
        compiler_params=pltpu.CompilerParams(vmem_limit_bytes=8 * 2**20),
    )(*made)
    return out.transpose(1, 0, 2), force, arrived.transpose(0, 2, 1, 3)


def solution(mesh):
    both = ("slab", "grp")
    in_specs = (
        P(None, both), P(None, None, both), P(None, both), P(both), P(both), P(both),
        P(both, None), P(both, None, None),
    )
    out_specs = (P(both, None, None), P(None, both), P(None, both, None, None))
    body = functools.partial(shards, mesh.shape["slab"], mesh.shape["grp"])
    return jax.shard_map(body, mesh=mesh, in_specs=in_specs, out_specs=out_specs, check_vma=False)
```
